32 devices in a mesh: section: 4 (over z), dp: 8 (over y, x, core).
Axes of the slice: x: 2, y: 2, z: 4, core: 2. Of those that a mesh axis runs over, the one named last changes fastest.
Arguments:
- byte_input: bfloat16 [32, 128, 768], P('dp'), may hold values from -6 to 6
- byte_ids: int32 [32, 128], P('dp'), may hold values from 0 to 255
- valid_bytes: int32 [32], P('dp'), may hold values from 32 to 128
- norm_gain: float32 [4, 2, 768], P('section'), may hold values from 0.5 to 1.5
- norm_bias: float32 [4, 2, 768], P('section'), may hold values from -3 to 3
- w_qkv: bfloat16 [4, 768, 2304], P('section'), may hold values from -0.21875 to 0.21875
- w_out: bfloat16 [4, 768, 768], P('section'), may hold values from -0.4375 to 0.4375
- w_up: bfloat16 [4, 768, 3072], P('section'), may hold values from -0.21875 to 0.21875
- w_down: bfloat16 [4, 3072, 768], P('section'), may hold values from -0.109375 to 0.109375
- patch_proj: bfloat16 [6144, 768], P(('section', 'dp')), may hold values from -0.078125 to 0.078125
- bridge: bfloat16 [6144, 768], P(('section', 'dp')), may hold values from -0.21875 to 0.21875
- byte_table: bfloat16 [256, 768], P(('section', 'dp')), may hold values from -6 to 6
- cotangent: bfloat16 [32, 128, 768], P('dp'), may hold values from -6 to 6
Outputs:
- mixed: bfloat16 [32, 128, 768], P('dp', 'section')
- grad_input: float32 [32, 128, 768], P('dp', 'section')
- grad_norm_gain: float32 [4, 2, 768], P('section', None, 'dp')
- grad_norm_bias: float32 [4, 2, 768], P('section', None, 'dp')
- grad_qkv: float32 [4, 768, 2304], P('section', 'dp')
- grad_out: float32 [4, 768, 768], P('section', 'dp')
- grad_up: float32 [4, 768, 3072], P('section', 'dp')
- grad_down: float32 [4, 3072, 768], P('section', 'dp')
- grad_patch: float32 [6144, 768], P(('section', 'dp'))
- grad_bridge: float32 [6144, 768], P(('section', 'dp'))
- grad_table: float32 [256, 768], P(('section', 'dp'))
The draws below stay inside these ranges and needn't reach their ends.
All inputs are finite; a program needn't handle non-finite values.
Results may differ from the reference program's by a relative error of at most 0.03.
Values may be sent and summed in bfloat16 or wider, within the bound.
No kernel may reach another device: no remote copies, remote signals or barrier semaphores. Data moves between devices by JAX's collectives and lax.ppermute only.
A program may use at most 640 MiB of HBM per device.

```python
import math
import jax
import jax.numpy as jnp
import numpy as np
from jax import lax

D = 768
HEADS = 12
HEAD = 64
FF = 3072
PATCH = 8
VOCAB = 256
LAYERS = 4
BYTES = 128
ITEMS = 32


def draw_valid_bytes(key, part):
    key = jax.random.fold_in(key, 11)
    first_key, second_key, third_key = jax.random.split(key, 3)
    counts = jax.random.randint(first_key, (ITEMS,), BYTES // 4, BYTES + 1)
    fullest = jax.random.randint(second_key, (), 0, ITEMS)
    emptiest = (fullest + 1 + jax.random.randint(third_key, (), 0, ITEMS - 1)) % ITEMS
    positions = jnp.arange(ITEMS)
    counts = jnp.where(positions == fullest, BYTES, counts)
    counts = jnp.where(positions == emptiest, BYTES // 4, counts)
    return counts.astype(jnp.int32)


def plant(array, key, least, top_value):
    extent = array.shape
    place = [jax.random.randint(jax.random.fold_in(key, axis), (), 0, extent[axis]) for axis in range(len(extent))]
    array = array.at[tuple(place)].set(least)
    longest = extent.index(max(extent))
    place[longest] = (place[longest] + 1) % extent[longest]
    return array.at[tuple(place)].set(top_value)


def level_of(stream_key, shape, shards, low, top_value):
    factor_of, own = 1.0, jax.random.fold_in(stream_key, 6)
    for axis_at, parts in shards:
        steps = jnp.exp(jax.random.uniform(jax.random.fold_in(own, axis_at), (parts,), jnp.float32, low / len(shards), top_value / len(shards)))
        factor_of = factor_of * jnp.repeat(steps, shape[axis_at] // parts).reshape([-1 if axis == axis_at else 1 for axis in range(len(shape))])
    return factor_of


def rank_bounds(number_of, slope):
    weights = [(1 << 20) // math.isqrt(standing ** slope) + 1 for standing in range(1, number_of + 1)]
    deviation = 1 + sum(weights) // (1 << 30)
    return np.cumsum(np.array([max(1, weight // deviation) for weight in weights]))


def ranked(stream_key, extent, amount, slope):
    grid = rank_bounds(amount, slope)
    lot = jax.random.randint(jax.random.fold_in(stream_key, 1), extent, 0, int(grid[amount - 1]))
    rank = jnp.searchsorted(jnp.asarray(grid, jnp.int32), lot, side="right")
    return jax.random.permutation(jax.random.fold_in(stream_key, 2), amount)[rank].astype(jnp.int32)


def bell_draw(own_key, dims, scale, reach, pieces=(), kind=jnp.bfloat16):
    array = jax.random.normal(own_key, dims, jnp.float32) * scale
    if len(pieces) > 0:
        array = level_of(own_key, dims, pieces, -0.22, 0.18) * array
    return jnp.clip(array, min=-reach, max=reach).astype(kind)


def setup_inputs(seed: int = 0) -> dict:
    streams_of = jax.random.split(jax.random.key(seed), 14)
    return {
        "byte_input": bell_draw(streams_of[0], (ITEMS, BYTES, D), 1.0, 6.0, ((0, 8),)),
        "byte_ids": plant(ranked(streams_of[1], (ITEMS, BYTES), VOCAB, 2), jax.random.fold_in(streams_of[1], 3), 0, VOCAB - 1).astype(jnp.int32),
        "valid_bytes": draw_valid_bytes(jax.random.fold_in(streams_of[13], 71), 0),
        "norm_gain": jnp.clip(1.0 + 0.1 * jax.random.normal(streams_of[3], (LAYERS, 2, D), jnp.float32), 0.5, 1.5),
        "norm_bias": bell_draw(streams_of[4], (LAYERS, 2, D), 0.3, 3.0, ((0, 4),), jnp.float32),
        "w_qkv": bell_draw(streams_of[5], (LAYERS, D, 3 * D), D ** -0.5, 0.21875, ((0, 4),)),
        "w_out": bell_draw(streams_of[6], (LAYERS, D, D), (D // 4) ** -0.5, 0.4375, ((0, 4),)),
        "w_up": bell_draw(streams_of[7], (LAYERS, D, FF), D ** -0.5, 0.21875, ((0, 4),)),
        "w_down": bell_draw(streams_of[8], (LAYERS, FF, D), FF ** -0.5, 0.109375, ((0, 4),)),
        "patch_proj": bell_draw(streams_of[9], (PATCH * D, D), (PATCH * D) ** -0.5, 0.078125, ((0, 32),)),
        "bridge": bell_draw(streams_of[10], (PATCH * D, D), D ** -0.5, 0.21875, ((0, 32),)),
        "byte_table": bell_draw(streams_of[11], (VOCAB, D), 1.0, 6.0, ((0, 32),)),
        "cotangent": bell_draw(streams_of[12], (ITEMS, BYTES, D), 1.0, 6.0, ((0, 8),)),
    }


@jax.custom_vjp
def low(v):
    return lax.optimization_barrier(v.astype(jnp.bfloat16)).astype(jnp.float32)

@jax.custom_vjp
def low_back(v):
    return v

def low_keep(v):
    return (low(v), None)

def low_pass(kept, grad):
    return (grad,)

def back_keep(v):
    return (v, None)

def back_low(kept, grad):
    return (low(grad),)
low.defvjp(low_keep, low_pass)
low_back.defvjp(back_keep, back_low)
EPSILON = 1e-05
MASK_FILL = -1e+30
EXACT = lax.Precision.HIGHEST

def layer_norm(stream, gain, shift):
    centred = stream - lax.optimization_barrier(jnp.mean(stream, axis=-1, keepdims=True))
    return centred * lax.rsqrt(lax.optimization_barrier(jnp.mean(centred * centred, axis=-1, keepdims=True)) + EPSILON) * gain + shift

def project(left, right):
    return jnp.matmul(left, right, precision=EXACT)

def block_ref(stream, gain, shift, weight_qkv, weight_out, weight_up, weight_down):
    seq_count, length, model_width = stream.shape
    first_low = low(layer_norm(stream, gain[0], shift[0]))
    qkv_rows = low(low_back(project(first_low, weight_qkv)))
    shaped = qkv_rows.reshape(seq_count, length, 3, HEADS, HEAD)
    queries, key_rows, value_rows = (shaped[:, :, 0], shaped[:, :, 1], shaped[:, :, 2])
    scores = jnp.einsum('blhd,bmhd->bhlm', queries, key_rows, precision=EXACT) * HEAD ** (-0.5)
    scores = low_back(scores)
    allowed = lax.broadcasted_iota(jnp.int32, (length, length), 0) >= lax.broadcasted_iota(jnp.int32, (length, length), 1)
    scores = jnp.where(allowed, scores, MASK_FILL)
    probability = low(jax.nn.softmax(scores, axis=-1))
    heads_out = jnp.einsum('bhlm,bmhd->blhd', probability, value_rows, precision=EXACT)
    attended = low(low_back(heads_out.reshape(seq_count, length, model_width)))
    mixed_stream = stream + low_back(project(attended, weight_out))
    second_low = low(layer_norm(mixed_stream, gain[1], shift[1]))
    hidden_pre = low_back(project(second_low, weight_up))
    active = low(jax.nn.gelu(hidden_pre))
    return mixed_stream + low_back(project(active, weight_down))

def forward(params, inputs, token_ids, keep_part):
    gain, shift, weight_qkv, weight_out, weight_up, weight_down, patch_w, bridge_w, table = params
    group_size, byte_count, model_width = inputs.shape
    patch_count = byte_count // PATCH
    stream = low_back(project(inputs.reshape(group_size, patch_count, PATCH * model_width), patch_w))
    for layer_index in range(2):
        stream = block_ref(stream, gain[layer_index], shift[layer_index], weight_qkv[layer_index], weight_out[layer_index], weight_up[layer_index], weight_down[layer_index])
        stream = low(low_back(stream))
    projected = project(stream, bridge_w.T).reshape(group_size, patch_count, PATCH, model_width)
    embedded = jnp.take(table, token_ids, axis=0).reshape(group_size, patch_count, PATCH, model_width)
    embedded = jnp.concatenate([jnp.zeros((group_size, patch_count, 1, model_width), jnp.float32), embedded[:, :, :-1]], axis=2)
    stream = low_back(embedded + projected).reshape(group_size * patch_count, PATCH, model_width)
    stream = block_ref(stream, gain[2], shift[2], weight_qkv[2], weight_out[2], weight_up[2], weight_down[2])
    stream = low(low_back(stream))
    stream = block_ref(stream, gain[3], shift[3], weight_qkv[3], weight_out[3], weight_up[3], weight_down[3])
    return stream.reshape(group_size, byte_count, model_width) * keep_part[..., None]

def reference(byte_input, byte_ids, valid_bytes, norm_gain, norm_bias, w_qkv, w_out, w_up, w_down, patch_proj, bridge, byte_table, cotangent):
    params = tuple((leaf.astype(jnp.float32) for leaf in (norm_gain, norm_bias, w_qkv, w_out, w_up, w_down, patch_proj, bridge, byte_table)))
    item_count, byte_count, model_width = byte_input.shape
    group_size = math.gcd(item_count, max(1, 4096 // byte_count))
    positions = lax.broadcasted_iota(jnp.int32, (item_count, byte_count), 1)
    keep_rows = (positions < valid_bytes[:, None]).astype(jnp.float32)

    def one_group(totals, index):
        offset = (index * group_size).astype(jnp.int32)
        inputs = lax.dynamic_slice_in_dim(byte_input, offset, group_size, 0).astype(jnp.float32)
        token_ids = lax.dynamic_slice_in_dim(byte_ids, offset, group_size, 0)
        keep_part = lax.dynamic_slice_in_dim(keep_rows, offset, group_size, 0)
        target = lax.dynamic_slice_in_dim(cotangent, offset, group_size, 0).astype(jnp.float32)
        result, pullback = jax.vjp(lambda weights, data: forward(weights, data, token_ids, keep_part), params, inputs)
        gradients, grad_inputs = pullback(target)
        totals = jax.tree.map(jnp.add, totals, gradients)
        return (totals, (result.astype(jnp.bfloat16), grad_inputs))
    initial = jax.tree.map(jnp.zeros_like, params)
    totals, outputs = lax.scan(one_group, initial, jnp.arange(item_count // group_size, dtype=jnp.int32))
    mixed = outputs[0].reshape(item_count, byte_count, model_width)
    grad_input = outputs[1].reshape(item_count, byte_count, model_width)
    return (mixed, grad_input, totals[0], totals[1], totals[2], totals[3], totals[4], totals[5], totals[6], totals[7], totals[8])
```

```python
import functools
import jax
import jax.numpy as jnp
from jax import lax
from jax.experimental import pallas as pl
from jax.experimental.pallas import tpu as pltpu
from jax.sharding import PartitionSpec as P

HEADS = 12
HEAD = 64
PATCH = 8
VOCAB = 256
EPSILON = 1e-05
MASK_FILL = -1e30
BF = jnp.bfloat16
F32 = jnp.float32
ANY = pl.BlockSpec(memory_space=pl.ANY)
VM = pl.BlockSpec(memory_space=pltpu.VMEM)
SM = pl.BlockSpec(memory_space=pltpu.SMEM)
NT = (((1,), (1,)), ((), ()))
TN = (((0,), (0,)), ((), ()))
ROOT = 0.7978845608028654
CUBE = 0.044715


def mm(left, right, dims=(((1,), (0,)), ((), ()))):
    return lax.dot_general(left, right, dims, preferred_element_type=F32)


def unit_rows(block):
    centred = block - jnp.mean(block, axis=-1, keepdims=True)
    inverse = lax.rsqrt(jnp.mean(centred * centred, axis=-1, keepdims=True) + EPSILON)
    return centred * inverse, inverse


def row_chunks(rows, body, step=64):
    step = min(step, rows)
    for at in range(rows // step):
        body(pl.ds(at * step, step))


def lane_low(rows):
    return lax.broadcasted_iota(jnp.int32, (rows, 128), 1) < HEAD


def two_heads(block):
    low = lane_low(block.shape[0])
    none = jnp.zeros_like(block)
    return jnp.concatenate([jnp.where(low, block, none), jnp.where(low, none, block)], axis=0)


def one_pair(block):
    half = block.shape[0] // 2
    return jnp.where(lane_low(half), block[:half], block[half:])


STORED = ("x", "a", "qkv", "p", "o", "x2", "c", "gp", "r")


def stored_shapes(rows, length, width, hidden):
    group = min(rows, 128)
    pairs = rows // group * (HEADS // 2)
    return {
        "x": ((rows, width), F32),
        "a": ((rows, width), BF),
        "qkv": ((rows, 3 * width), BF),
        "p": ((pairs, 2 * group, group), BF),
        "o": ((rows, width), BF),
        "x2": ((rows, width), F32),
        "c": ((rows, width), BF),
        "gp": ((rows, hidden), BF),
        "r": ((rows, hidden), BF),
    }


def fwd_kernel(rows, length, stride, lead, *refs):
    (ctrl, x_ref, gain, bias, wqkv_h, wout_h, wup_h, wdown_h) = refs[:8]
    refs = refs[8 + lead:]
    y_ref = refs[0]
    out = dict(zip(STORED, refs[1:10]))
    buf = dict(zip(STORED[1:], refs[10:18]))
    wqkv, wout, wup, wdown, wsem, osem = refs[18:]
    width = x_ref.shape[1]
    hidden = wup.shape[1]
    group = min(rows, 128)

    @pl.when(ctrl[0] == 1)
    def run():
        index = ctrl[1]
        loads = [
            pltpu.make_async_copy(wqkv_h, wqkv, wsem.at[0]),
            pltpu.make_async_copy(wout_h, wout, wsem.at[1]),
            pltpu.make_async_copy(wup_h, wup, wsem.at[2]),
            pltpu.make_async_copy(wdown_h, wdown, wsem.at[3]),
        ]
        for load in loads:
            load.start()
        saves = []

        def save(name, source=None):
            target = out[name]
            extent = target.shape[0] // (target.shape[0] // (buf[name] if source is None else source).shape[0])
            copy = pltpu.make_async_copy(
                buf[name] if source is None else source,
                target.at[pl.ds(index * extent, extent)],
                osem.at[len(saves)],
            )
            copy.start()
            saves.append(copy)

        save("x", x_ref)

        def norm_one(at):
            unit, _ = unit_rows(x_ref[at, :])
            buf["a"][at, :] = (unit * gain[0:1, :] + bias[0:1, :]).astype(BF)

        row_chunks(rows, norm_one)
        save("a")
        loads[0].wait()
        for at in range(0, 3 * width, 256):
            buf["qkv"][:, at:at + 256] = mm(buf["a"][...], wqkv[:, at:at + 256]).astype(BF)
        save("qkv")

        row = lax.broadcasted_iota(jnp.int32, (2 * group, group), 0) % group
        col = lax.broadcasted_iota(jnp.int32, (2 * group, group), 1)
        if stride == 1:
            same = col // length == row // length
        else:
            same = col % stride == row % stride
        allowed = (col <= row) & same

        def attend(which, carry):
            at = pl.ds(pl.multiple_of(which * group, group), group)
            for pair in range(HEADS // 2):
                lanes = pair * 128
                queries = buf["qkv"][at, lanes:lanes + 128] * jnp.asarray(HEAD ** -0.5, BF)
                keys = buf["qkv"][at, width + lanes:width + lanes + 128]
                values = buf["qkv"][at, 2 * width + lanes:2 * width + lanes + 128]
                scores = jnp.where(allowed, mm(two_heads(queries), keys, NT), MASK_FILL)
                weight = jnp.exp(scores - jnp.max(scores, axis=-1, keepdims=True))
                chance = (weight / jnp.sum(weight, axis=-1, keepdims=True)).astype(BF)
                buf["p"][which * (HEADS // 2) + pair] = chance
                buf["o"][at, lanes:lanes + 128] = one_pair(mm(chance, values)).astype(BF)
            return carry

        lax.fori_loop(0, rows // group, attend, 0)
        save("p")
        save("o")
        loads[1].wait()
        for at in range(0, width, 256):
            buf["x2"][:, at:at + 256] = x_ref[:, at:at + 256] + mm(buf["o"][...], wout[:, at:at + 256])
        save("x2")

        def norm_two(at):
            unit, _ = unit_rows(buf["x2"][at, :])
            buf["c"][at, :] = (unit * gain[1:2, :] + bias[1:2, :]).astype(BF)

        row_chunks(rows, norm_two)
        save("c")
        loads[2].wait()
        for at in range(0, hidden, 256):
            pre = mm(buf["c"][...], wup[:, at:at + 256])
            square = pre * pre
            bent = jnp.tanh(ROOT * (pre + CUBE * square * pre))
            share = 0.5 * (1.0 + bent)
            buf["r"][:, at:at + 256] = (pre * share).astype(BF)
            slope = share + (0.5 * ROOT) * pre * (1.0 - bent * bent) * (1.0 + (3 * CUBE) * square)
            buf["gp"][:, at:at + 256] = slope.astype(BF)
        save("gp")
        save("r")
        loads[3].wait()
        for at in range(0, width, 256):
            y_ref[:, at:at + 256] = (
                buf["x2"][:, at:at + 256] + mm(buf["r"][...], wdown[:, at:at + 256])
            ).astype(BF)
        for copy in saves:
            copy.wait()


def block_fwd(ctrl, x, gain, bias, weights, stored, total, length, stride, name):
    rows, width = x.shape
    hidden = weights[2].shape[1]
    shapes = stored_shapes(rows, length, width, hidden)
    times = total // rows
    full = [
        jax.ShapeDtypeStruct((shapes[k][0][0] * times,) + shapes[k][0][1:], shapes[k][1]) for k in STORED
    ]
    lead = 0 if stored is None else len(STORED)
    result = pl.pallas_call(
        functools.partial(fwd_kernel, rows, length, stride, lead),
        out_shape=[jax.ShapeDtypeStruct((rows, width), BF)] + full,
        in_specs=[SM, VM, VM, VM, ANY, ANY, ANY, ANY] + [ANY] * lead,
        out_specs=[VM] + [ANY] * len(STORED),
        scratch_shapes=[pltpu.VMEM(*shapes[k]) for k in STORED[1:]]
        + [pltpu.VMEM(w.shape, w.dtype) for w in weights]
        + [pltpu.SemaphoreType.DMA((4,)), pltpu.SemaphoreType.DMA((len(STORED),))],
        input_output_aliases={8 + i: 1 + i for i in range(lead)},
        compiler_params=pltpu.CompilerParams(vmem_limit_bytes=56 << 20),
        name=name,
    )(ctrl, x, gain, bias, *weights, *(() if stored is None else stored))
    return result[0], tuple(result[1:])


GRADS = ("dz", "du", "dA", "dqkv")
USED = ("x", "qkv", "p", "x2", "gp")


def norm_back_rows(grad, unit, inverse, gain_row):
    scaled = grad * gain_row
    return inverse * (
        scaled
        - jnp.mean(scaled, axis=-1, keepdims=True)
        - unit * jnp.mean(scaled * unit, axis=-1, keepdims=True)
    )


def bwd_kernel(rows, length, lead, *refs):
    (ctrl, dy_ref, gain, wqkv_h, wout_h, wup_h, wdown_h) = refs[:7]
    src = dict(zip(USED, refs[7:12]))
    refs = refs[12 + lead:]
    dx_ref, gn_ref = refs[:2]
    out = dict(zip(GRADS, refs[2:6]))
    buf = dict(zip(USED, refs[6:11]))
    grd = dict(zip(GRADS[1:], refs[11:14]))
    do_s, dx2_s, wqkv, wout, wup, wdown, wsem, rsem, osem = refs[14:]
    width = dx_ref.shape[1]
    hidden = wup.shape[1]
    group = min(rows, 128)

    @pl.when(ctrl[0] == 1)
    def run():
        index = ctrl[1]
        reads = {}

        def read(name, at):
            extent = buf[name].shape[0]
            reads[name] = pltpu.make_async_copy(
                src[name].at[pl.ds(index * extent, extent)], buf[name], rsem.at[at]
            )
            reads[name].start()

        loads = [
            pltpu.make_async_copy(wdown_h, wdown, wsem.at[0]),
            pltpu.make_async_copy(wup_h, wup, wsem.at[1]),
            pltpu.make_async_copy(wout_h, wout, wsem.at[2]),
            pltpu.make_async_copy(wqkv_h, wqkv, wsem.at[3]),
        ]
        loads[0].start()
        read("gp", 0)
        loads[1].start()
        read("x2", 1)
        loads[2].start()
        read("qkv", 2)
        read("p", 3)
        loads[3].start()
        read("x", 4)
        saves = []

        def save(name, source=None):
            source = grd[name] if source is None else source
            extent = source.shape[0]
            copy = pltpu.make_async_copy(
                source, out[name].at[pl.ds(index * extent, extent)], osem.at[len(saves)]
            )
            copy.start()
            saves.append(copy)

        save("dz", dy_ref)
        loads[0].wait()
        reads["gp"].wait()
        for at in range(0, hidden, 256):
            part = mm(dy_ref[...], wdown[at:at + 256, :], NT)
            grd["du"][:, at:at + 256] = (part * buf["gp"][:, at:at + 256].astype(F32)).astype(BF)
        save("du")
        loads[1].wait()
        reads["x2"].wait()
        for at in range(0, width, 256):
            dx2_s[:, at:at + 256] = mm(grd["du"][...], wup[at:at + 256, :], NT)
        gn_ref[...] = jnp.zeros_like(gn_ref)

        def back_two(at):
            unit, inverse = unit_rows(buf["x2"][at, :])
            grad = dx2_s[at, :]
            gn_ref[1:2, :] += jnp.sum(grad * unit, axis=0, keepdims=True)
            gn_ref[3:4, :] += jnp.sum(grad, axis=0, keepdims=True)
            mixed = dy_ref[at, :].astype(F32) + norm_back_rows(grad, unit, inverse, gain[1:2, :])
            dx2_s[at, :] = mixed
            grd["dA"][at, :] = mixed.astype(BF)

        row_chunks(rows, back_two)
        save("dA")
        loads[2].wait()
        for at in range(0, width, 256):
            do_s[:, at:at + 256] = mm(grd["dA"][...], wout[at:at + 256, :], NT).astype(BF)
        reads["qkv"].wait()
        reads["p"].wait()

        def attend(which, carry):
            at = pl.ds(pl.multiple_of(which * group, group), group)
            for pair in range(HEADS // 2):
                lanes = pair * 128
                queries = two_heads(buf["qkv"][at, lanes:lanes + 128] * jnp.asarray(HEAD ** -0.5, BF))
                keys = buf["qkv"][at, width + lanes:width + lanes + 128]
                values = buf["qkv"][at, 2 * width + lanes:2 * width + lanes + 128]
                grads = two_heads(do_s[at, lanes:lanes + 128])
                chance = buf["p"][which * (HEADS // 2) + pair]
                wide = chance.astype(F32)
                slope = mm(grads, values, NT)
                weighed = slope * wide
                total = jnp.sum(weighed, axis=-1, keepdims=True)
                scores = (weighed - wide * total).astype(BF)
                dq = one_pair(mm(scores, keys)) * HEAD ** -0.5
                dk = mm(scores, queries, TN)
                dv = mm(chance, grads, TN)
                grd["dqkv"][at, lanes:lanes + 128] = dq.astype(BF)
                grd["dqkv"][at, width + lanes:width + lanes + 128] = dk.astype(BF)
                grd["dqkv"][at, 2 * width + lanes:2 * width + lanes + 128] = dv.astype(BF)
            return carry

        lax.fori_loop(0, rows // group, attend, 0)
        save("dqkv")
        loads[3].wait()
        reads["x"].wait()
        for at in range(0, width, 256):
            buf["x2"][:, at:at + 256] = mm(grd["dqkv"][...], wqkv[at:at + 256, :], NT)

        def back_one(at):
            unit, inverse = unit_rows(buf["x"][at, :])
            grad = buf["x2"][at, :]
            gn_ref[0:1, :] += jnp.sum(grad * unit, axis=0, keepdims=True)
            gn_ref[2:3, :] += jnp.sum(grad, axis=0, keepdims=True)
            dx_ref[at, :] = (
                dx2_s[at, :] + norm_back_rows(grad, unit, inverse, gain[0:1, :])
            ).astype(BF)

        row_chunks(rows, back_one)
        for copy in saves:
            copy.wait()


def block_bwd(ctrl, dy, gain, weights, stored, grads, total, length, name):
    rows, width = dy.shape
    hidden = weights[2].shape[1]
    shapes = stored_shapes(rows, length, width, hidden)
    pick = dict(zip(STORED, stored))
    gshape = {"dz": width, "du": hidden, "dA": width, "dqkv": 3 * width}
    lead = 0 if grads is None else len(GRADS)
    result = pl.pallas_call(
        functools.partial(bwd_kernel, rows, length, lead),
        out_shape=[jax.ShapeDtypeStruct((rows, width), BF), jax.ShapeDtypeStruct((8, width), F32)]
        + [jax.ShapeDtypeStruct((total, gshape[k]), BF) for k in GRADS],
        in_specs=[SM, VM, VM, ANY, ANY, ANY, ANY] + [ANY] * (len(USED) + lead),
        out_specs=[VM, VM] + [ANY] * len(GRADS),
        scratch_shapes=[pltpu.VMEM(*shapes[k]) for k in USED]
        + [pltpu.VMEM((rows, gshape[k]), BF) for k in GRADS[1:]]
        + [pltpu.VMEM((rows, width), BF), pltpu.VMEM((rows, width), F32)]
        + [pltpu.VMEM(w.shape, w.dtype) for w in weights]
        + [
            pltpu.SemaphoreType.DMA((4,)),
            pltpu.SemaphoreType.DMA((len(USED),)),
            pltpu.SemaphoreType.DMA((len(GRADS),)),
        ],
        input_output_aliases={12 + i: 2 + i for i in range(lead)},
        compiler_params=pltpu.CompilerParams(vmem_limit_bytes=56 << 20),
        name=name,
    )(ctrl, dy, gain, *weights, *(pick[k] for k in USED), *(() if grads is None else grads))
    return result[0], result[1], tuple(result[2:])


def product_kernel(place_ref, left, right, mine, theirs, tiles, sems):
    depth, extent = left.shape[1], mine.shape[1]
    step = tiles.shape[2]
    copies = {}
    for tile in range(right.shape[1] // step):
        slot = tile % 2
        at = pl.ds(tile * step, step)
        for copy in copies.get(slot, ()):
            copy.wait()
        tiles[slot] = mm(left[...], right[:, at], TN).astype(BF)
        copies[slot] = []
        for shard in range(depth // extent):
            source = tiles.at[slot, pl.ds(shard * extent, extent)]
            other = place_ref[0] ^ shard
            same = (other & 1) == 0
            to_mine = pltpu.make_async_copy(source, mine.at[other >> 1, :, at], sems.at[slot, shard])
            to_theirs = pltpu.make_async_copy(source, theirs.at[other >> 1, :, at], sems.at[slot, shard])

            @pl.when(same)
            def keep():
                to_mine.start()

            @pl.when(jnp.logical_not(same))
            def give():
                to_theirs.start()

            copies[slot].append(to_mine)
    for group in copies.values():
        for copy in group:
            copy.wait()


def products(place, left, right, shards, name):
    depth, wide = left.shape[1], right.shape[1]
    half = jax.ShapeDtypeStruct((shards // 2, depth // shards, wide), BF)
    return pl.pallas_call(
        product_kernel,
        out_shape=[half, half],
        in_specs=[SM, VM, VM],
        out_specs=[ANY, ANY],
        scratch_shapes=[pltpu.VMEM((2, depth, 256), BF), pltpu.SemaphoreType.DMA((2, shards))],
        compiler_params=pltpu.CompilerParams(vmem_limit_bytes=40 << 20),
        name=name,
    )(place.reshape(1).astype(jnp.int32), left, right)


def swap(block, mask, planes):
    shards = lax.axis_size("dp")
    pairs = [(s * shards + i, s * shards + (i ^ mask)) for s in planes for i in range(shards)]
    return lax.ppermute(block, ("section", "dp"), pairs)


def gather_rows(block, planes):
    shards = lax.axis_size("dp")
    place = lax.axis_index("dp")
    extent = block.shape[0]
    if shards > 8:
        return lax.all_gather(block, "dp", axis=0, tiled=True)
    same = [block] + [swap(block, mask, planes) for mask in range(2, shards, 2)]
    other = swap(jnp.concatenate(same, axis=0), 1, planes)
    whole = jnp.zeros((shards * extent, block.shape[1]), block.dtype)
    for at, piece in enumerate(same):
        whole = lax.dynamic_update_slice(whole, piece, ((place ^ (2 * at)) * extent, 0))
    for at in range(shards // 2):
        piece = other[at * extent:(at + 1) * extent]
        whole = lax.dynamic_update_slice(whole, piece, ((place ^ (2 * at) ^ 1) * extent, 0))
    return whole


def reduce_shards(pair, planes):
    mine, theirs = pair
    came = swap(theirs, 1, planes)
    half = mine.shape[1] // 2

    def first(mask, lower):
        rows = slice(0, half) if lower else slice(half, None)
        return mine[mask, rows].astype(F32) + came[mask, rows].astype(F32)

    lows = swap(jnp.stack([first(1, True), first(3, True)]).astype(BF), 2, planes)
    highs = swap(jnp.stack([first(2, False), first(3, False)]).astype(BF), 4, planes)
    low = swap((first(2, True) + lows[1].astype(F32)).astype(BF), 4, planes)
    high = swap((first(1, False) + highs[1].astype(F32)).astype(BF), 2, planes)
    return jnp.concatenate(
        [
            first(0, True) + lows[0].astype(F32) + low.astype(F32),
            first(0, False) + highs[0].astype(F32) + high.astype(F32),
        ],
        axis=0,
    )


def weight_grads(kept, slopes, planes):
    shards = lax.axis_size("dp")
    place = lax.axis_index("dp")
    results = []
    for left, right in zip(kept, slopes):
        if shards == 8:
            results.append(reduce_shards(products(place, left, right, shards, "weight_grad"), planes))
        else:
            whole = mm(left, right, TN).astype(BF)
            results.append(lax.psum_scatter(whole, "dp", scatter_dimension=0, tiled=True).astype(F32))
    return results


def hop(block, source, target):
    return lax.ppermute(block, "section", [(source, target)])


def on_device(
    byte_input,
    byte_ids,
    valid_bytes,
    norm_gain,
    norm_bias,
    w_qkv,
    w_out,
    w_up,
    w_down,
    patch_proj,
    bridge,
    byte_table,
    cotangent,
):
    rank = lax.axis_index("section")
    place = lax.axis_index("dp")
    sections = lax.axis_size("section")
    shards = lax.axis_size("dp")
    items, byte_count, width = byte_input.shape
    hidden = w_up.shape[2]
    patch_count = byte_count // PATCH
    rows = items * byte_count
    small = items * patch_count
    gain, bias = norm_gain[0], norm_bias[0]
    weights = (w_qkv[0], w_out[0], w_up[0], w_down[0])
    half, last = sections // 2, sections - 1
    every = range(sections)
    global_planes, local_planes = range(half), range(half, sections)
    is_first, is_second, is_bridge, is_last = rank == 0, rank == 1, rank == half, rank == last
    is_global = rank < half
    parts = 2 if items % 2 == 0 else 1
    chunk = rows // parts
    own_bytes = PATCH // sections
    own = own_bytes * width
    per = VOCAB // sections

    def control(active, index):
        return jnp.stack([active, index]).astype(jnp.int32)

    zero = jnp.zeros((), jnp.int32)

    patch_rows = gather_rows(patch_proj, every)
    patches = byte_input.reshape(small, PATCH * width)
    patches = lax.dynamic_slice_in_dim(patches, rank * own, own, 1)
    share = mm(patches, patch_rows)
    sent = share.astype(BF)
    stream = share + sum(hop(sent, source, 0).astype(F32) for source in range(1, sections))

    entry_rows = lax.optimization_barrier((jnp.concatenate([bridge, byte_table], axis=0), patch_rows))[0]
    shared = gather_rows(entry_rows, every).reshape(shards, -1, width)
    bridge_rows = shared[:, :own // shards].reshape(own, width)
    table_rows = shared[:, own // shards:].reshape(per, width)
    table = jnp.concatenate([table_rows if s == half else hop(table_rows, s, half) for s in every], axis=0)

    def by_byte(block):
        shaped = block.reshape((items, patch_count, PATCH) + block.shape[2:])
        return jnp.swapaxes(shaped, 1, 2)

    ids = by_byte(byte_ids)
    before = jnp.concatenate([jnp.full_like(ids[:, :1], -1), ids[:, :-1]], axis=1).reshape(rows)
    one_hot = (before[:, None] == lax.broadcasted_iota(jnp.int32, (rows, VOCAB), 1)).astype(BF)
    positions = lax.broadcasted_iota(jnp.int32, (items, byte_count), 1)
    keep = by_byte((positions < valid_bytes[:, None]).astype(BF)).reshape(rows, 1)
    target = by_byte(cotangent).reshape(rows, width) * keep
    embedded = mm(one_hot, table)

    def global_forward(start):
        first_out, kept = block_fwd(
            control(is_first, zero), start, gain, bias, weights, None, small, patch_count, 1, "global_fwd_one"
        )
        received = lax.ppermute(first_out, ("section", "dp"), [(i, shards + i) for i in range(shards)])
        second_out, kept = block_fwd(
            control(is_second, zero),
            received.astype(F32),
            gain,
            bias,
            weights,
            kept,
            small,
            patch_count,
            1,
            "global_fwd_two",
        )
        return second_out, kept

    def global_idle(start):
        shapes = stored_shapes(small, patch_count, width, hidden)
        return jnp.zeros((small, width), BF), tuple(jnp.zeros(*shapes[k]) for k in STORED)

    second_out, global_store = lax.cond(is_global, global_forward, global_idle, stream)
    summary = jnp.where(is_second, second_out, sum(hop(second_out, 1, s) for s in every if s != 1))

    global_pick = dict(zip(STORED, global_store))
    columns = [
        global_pick[key].reshape(small, shards, -1).transpose(1, 0, 2) for key in KEPT
    ]
    columns = lax.optimization_barrier((jnp.concatenate(columns, axis=2), summary))[0]
    global_columns = lax.all_to_all(columns, "dp", 0, 0, tiled=True)

    projected = jnp.stack(
        [mm(summary, bridge_rows[b * width:(b + 1) * width], NT).astype(BF) for b in range(own_bytes)]
    )
    projected = jnp.concatenate([projected if s == half else hop(projected, s, half) for s in every], axis=0)
    projected = jnp.swapaxes(projected.reshape(PATCH, items, patch_count, width), 0, 1).reshape(rows, width)
    entered = embedded + projected.astype(F32)

    def local_blocks(entered, target):
        store, grads, back = None, None, None
        finals, entries, norms = [], [], []
        coming = jnp.zeros((chunk, width), BF)
        up = [(half * shards + i, last * shards + i) for i in range(shards)]
        down = [(b, a) for a, b in up]
        for tick in range(parts + 2):
            if tick <= parts:
                active = (is_bridge & (tick < parts)) | (is_last & (tick >= 1))
                index = jnp.where(is_last, tick - 1, tick)
                lead = entered[tick * chunk:(tick + 1) * chunk] if tick < parts else entered[:chunk]
                rows_in = jnp.where(is_last, coming.astype(F32), lead)
                result, store = block_fwd(
                    control(active, index),
                    rows_in,
                    gain,
                    bias,
                    weights,
                    store,
                    rows,
                    PATCH,
                    patch_count,
                    "local_fwd_%d" % tick,
                )
                if tick < parts:
                    coming = lax.ppermute(result, ("section", "dp"), up)
                if tick >= 1:
                    finals.append(result)
            if tick >= 1:
                active = (is_last & (tick <= parts)) | (is_bridge & (tick >= 2))
                index = jnp.where(is_last, tick - 1, tick - 2)
                at = min(tick - 1, parts - 1) * chunk
                slope = target[at:at + chunk]
                if back is not None:
                    slope = jnp.where(is_last, slope, back)
                result, norm, grads = block_bwd(
                    control(active, index), slope, gain, weights, store, grads, rows, PATCH, "local_bwd_%d" % tick
                )
                norms.append(jnp.where(active, norm, 0.0))
                store, result = lax.optimization_barrier((store, result))
                if tick <= parts:
                    back = lax.ppermute(result, ("section", "dp"), down)
                if tick >= 2:
                    entries.append(result)
        pick = dict(zip(STORED, store))
        slopes = dict(zip(GRADS, grads))
        return (
            jnp.concatenate(finals, axis=0),
            jnp.concatenate(entries, axis=0),
            sum(norms),
            tuple(pick[k] for k in KEPT),
            tuple(slopes[k] for k in SLOPES),
        )

    wide = {"r": hidden, "du": hidden, "dqkv": 3 * width}

    def local_idle(entered, target):
        blank = jnp.zeros((rows, width), BF)
        return (
            blank,
            blank,
            jnp.zeros((8, width), F32),
            tuple(jnp.zeros((rows, wide.get(k, width)), BF) for k in KEPT),
            tuple(jnp.zeros((rows, wide.get(k, width)), BF) for k in SLOPES),
        )

    final, entry, norm, local_kept, local_slopes = lax.cond(
        is_global, local_idle, local_blocks, entered, target
    )

    entry = jnp.swapaxes(entry.reshape(items, PATCH, small // items, width), 0, 1)
    entry = entry.reshape(sections, own_bytes, small, width)
    slope = select_section(entry, rank, half, sections)
    part = sum(mm(slope[b], bridge_rows[b * width:(b + 1) * width]) for b in range(own_bytes))
    sent = part.astype(BF)
    arriving = (part + sum(hop(sent, s, 1).astype(F32) for s in every if s != 1)).astype(BF)

    def global_backward(operands):
        arriving, norm, kept, slopes = operands
        second_back, norm_two, grads = block_bwd(
            control(is_second, zero), arriving, gain, weights, global_store, None, small, patch_count, "global_bwd_two"
        )
        coming = lax.ppermute(second_back, ("section", "dp"), [(shards + i, i) for i in range(shards)])
        start_back, norm_one, grads = block_bwd(
            control(is_first, zero), coming, gain, weights, global_store, grads, small, patch_count, "global_bwd_one"
        )
        norm = jnp.where(is_first, norm_one, jnp.where(is_second, norm_two, 0.0))
        grads = dict(zip(GRADS, grads))
        blank = [jnp.zeros((kept[i].shape[1] // shards, slopes[i].shape[1]), F32) for i in range(2)]
        return start_back, norm, tuple(grads[k] for k in SLOPES), tuple(blank)

    def local_weights_one(operands):
        arriving, norm, kept, slopes = operands
        made = weight_grads(kept[:2], slopes[:2], local_planes)
        blank = tuple(jnp.zeros((small, wide.get(k, width)), BF) for k in SLOPES)
        return jnp.zeros((small, width), BF), norm, blank, tuple(made)

    start_back, norm, global_slopes, made_one = lax.cond(
        is_global, global_backward, local_weights_one, (arriving, norm, local_kept, local_slopes)
    )
    norm_sum = lax.psum_scatter(norm[:4], "dp", scatter_dimension=1, tiled=True)
    start_all = jnp.where(is_first, start_back, sum(hop(start_back, 0, s) for s in range(1, sections)))

    def global_weights(operands):
        global_slopes, made_one, kept, slopes = operands
        packed = gather_rows(jnp.concatenate(global_slopes, axis=1), global_planes)
        results = []
        at, from_column = 0, 0
        for key, slope_key in zip(KEPT, SLOPES):
            columns = wide.get(slope_key, width)
            extent = wide.get(key, width) // shards
            left = global_columns[:, :, from_column:from_column + extent].reshape(shards * small, extent)
            results.append(mm(left, packed[:, at:at + columns], TN))
            at += columns
            from_column += extent
        return tuple(results)

    def local_weights_two(operands):
        global_slopes, made_one, kept, slopes = operands
        return tuple(made_one) + tuple(weight_grads(kept[2:], slopes[2:], local_planes))

    made = lax.cond(
        is_global, global_weights, local_weights_two, (global_slopes, made_one, local_kept, local_slopes)
    )
    made = dict(zip(KEPT, made))

    table_part = mm(one_hot, entry_flat(entry, items, rows, width), TN).astype(BF).reshape(sections, per, width)
    table_part = select_section(table_part, rank, half, sections)
    columns = jnp.swapaxes(slope, 0, 1).reshape(small, shards, own // shards).transpose(1, 0, 2)
    packed = jnp.concatenate([columns, table_part.reshape(shards, small, -1)], axis=2)
    swapped = lax.all_to_all(packed, "dp", 0, 0, tiled=True)
    columns = swapped[:, :, :own // shards].reshape(shards * small, own // shards)
    grad_bridge = mm(columns, lax.all_gather(summary, "dp", axis=0, tiled=True), TN)
    grad_table = jnp.sum(swapped[:, :, own // shards:].astype(F32), axis=0).reshape(per // shards, width)

    patch_shards = patches.reshape(small, shards, own // shards).transpose(1, 0, 2)
    patch_columns = lax.all_to_all(patch_shards, "dp", 0, 0, tiled=True).reshape(shards * small, own // shards)
    grad_patch = mm(patch_columns, lax.all_gather(start_all, "dp", axis=0, tiled=True), TN)

    inputs = mm(start_all, patch_rows, NT).astype(BF)
    inputs = inputs.reshape(items, sections, patch_count // sections, own).transpose(1, 0, 2, 3)
    inputs = lax.all_to_all(inputs, "section", 0, 0, tiled=True)
    grad_input = inputs.transpose(1, 2, 0, 3).reshape(items, byte_count // sections, width).astype(F32)

    mixed = (final * keep).reshape(items, PATCH, sections, patch_count // sections, width)
    mixed = select_section(mixed.transpose(2, 0, 1, 3, 4), rank, last, sections)
    mixed = jnp.swapaxes(mixed, 1, 2).reshape(items, byte_count // sections, width)
    return (
        mixed,
        grad_input,
        norm_sum[None, 0:2],
        norm_sum[None, 2:4],
        made["a"][None],
        made["o"][None],
        made["c"][None],
        made["r"][None],
        grad_patch,
        grad_bridge,
        grad_table,
    )


KEPT = ("r", "c", "o", "a")
SLOPES = ("dz", "du", "dA", "dqkv")


def entry_flat(entry, items, rows, width):
    shaped = entry.reshape(PATCH, items, -1, width)
    return jnp.swapaxes(shaped, 0, 1).reshape(rows, width)


def select_section(blocks, rank, source, sections):
    result = blocks[source]
    for section in range(sections):
        if section != source:
            result = jnp.where(rank == section, hop(blocks[section], source, section), result)
    return result


def solution(mesh):
    return jax.shard_map(
        on_device,
        mesh=mesh,
        in_specs=(
            P("dp", None, None),
            P("dp", None),
            P("dp"),
            P("section", None, None),
            P("section", None, None),
            P("section", None, None),
            P("section", None, None),
            P("section", None, None),
            P("section", None, None),
            P(("section", "dp"), None),
            P(("section", "dp"), None),
            P(("section", "dp"), None),
            P("dp", None, None),
        ),
        out_specs=(
            P("dp", "section", None),
            P("dp", "section", None),
            P("section", None, "dp"),
            P("section", None, "dp"),
            P("section", "dp", None),
            P("section", "dp", None),
            P("section", "dp", None),
            P("section", "dp", None),
            P(("section", "dp"), None),
            P(("section", "dp"), None),
            P(("section", "dp"), None),
        ),
        check_vma=False,
    )
```

```python
import functools
import jax
import jax.numpy as jnp
from jax import lax
from jax.experimental import pallas as pl
from jax.experimental.pallas import tpu as pltpu
from jax.sharding import PartitionSpec as P

HEADS = 12
HEAD = 64
PATCH = 8
VOCAB = 256
EPSILON = 1e-05
MASK_FILL = -1e30
BF = jnp.bfloat16
F32 = jnp.float32
ANY = pl.BlockSpec(memory_space=pl.ANY)
VM = pl.BlockSpec(memory_space=pltpu.VMEM)
SM = pl.BlockSpec(memory_space=pltpu.SMEM)
NT = (((1,), (1,)), ((), ()))
TN = (((0,), (0,)), ((), ()))
ROOT = 0.7978845608028654
CUBE = 0.044715
STORED = ("x", "a", "qkv", "p", "o", "x2", "c", "gp", "r")
GRADS = ("dz", "du", "dA", "dqkv")
USED = ("x", "qkv", "p", "x2", "gp")
KEPT = ("r", "c", "o", "a")


def mm(left, right, dims=(((1,), (0,)), ((), ()))):
    return lax.dot_general(left, right, dims, preferred_element_type=F32)


def unit_rows(block):
    centred = block - jnp.mean(block, axis=-1, keepdims=True)
    inverse = lax.rsqrt(jnp.mean(centred * centred, axis=-1, keepdims=True) + EPSILON)
    return centred * inverse, inverse


def row_chunks(rows, body, step=64):
    step = min(step, rows)
    for at in range(rows // step):
        body(pl.ds(at * step, step))


def lane_low(rows):
    return lax.broadcasted_iota(jnp.int32, (rows, 128), 1) < HEAD


def two_heads(block):
    low = lane_low(block.shape[0])
    none = jnp.zeros_like(block)
    return jnp.concatenate([jnp.where(low, block, none), jnp.where(low, none, block)], axis=0)


def one_pair(block):
    half = block.shape[0] // 2
    return jnp.where(lane_low(half), block[:half], block[half:])


def stored_shapes(rows, width, hidden):
    group = min(rows, 128)
    pairs = rows // group * (HEADS // 2)
    return {
        "x": ((rows, width), F32),
        "a": ((rows, width), BF),
        "qkv": ((rows, 3 * width), BF),
        "p": ((pairs, 2 * group, group), BF),
        "o": ((rows, width), BF),
        "x2": ((rows, width), F32),
        "c": ((rows, width), BF),
        "gp": ((rows, hidden), BF),
        "r": ((rows, hidden), BF),
    }


def own_rows(ref, rows, index):
    return ref if ref.shape[0] == rows else ref.at[pl.ds(index * rows, rows)]


def fwd_kernel(rows, length, stride, counts, lead, *refs):
    ctrl = refs[0]
    groups = (refs[1:1 + counts[0]], refs[1 + counts[0]:1 + sum(counts)])
    refs = refs[1 + sum(counts):]
    gain, bias, wqkv_h, wout_h, wup_h, wdown_h = refs[:6]
    refs = refs[6 + lead:]
    y_ref = refs[0]
    out = dict(zip(STORED, refs[1:10]))
    buf = dict(zip(STORED, refs[10:19]))
    stage = refs[19:19 + sum(counts)]
    wqkv, wout, wup, wdown, xsem, wsem, osem = refs[19 + sum(counts):]
    stages = (stage[:counts[0]], stage[counts[0]:])
    x_ref = buf["x"]
    width = x_ref.shape[1]
    hidden = wup.shape[1]
    group = min(rows, 128)

    @pl.when(ctrl[0] == 1)
    def run():
        index = ctrl[1]
        for which in range(2):
            if counts[which] == 0:
                continue

            @pl.when(ctrl[2] == which)
            def bring():
                for at, (ref, to) in enumerate(zip(groups[which], stages[which])):
                    pltpu.make_async_copy(own_rows(ref, rows, index), to, xsem.at[at]).start()

        loads = [
            pltpu.make_async_copy(wqkv_h, wqkv, wsem.at[0]),
            pltpu.make_async_copy(wout_h, wout, wsem.at[1]),
            pltpu.make_async_copy(wup_h, wup, wsem.at[2]),
            pltpu.make_async_copy(wdown_h, wdown, wsem.at[3]),
        ]
        loads[0].start()
        for which in range(2):
            if counts[which] == 0:
                continue

            @pl.when(ctrl[2] == which)
            def total():
                for at, (ref, to) in enumerate(zip(groups[which], stages[which])):
                    pltpu.make_async_copy(own_rows(ref, rows, index), to, xsem.at[at]).wait()

                def add(at):
                    x_ref[at, :] = sum(to[at, :].astype(F32) for to in stages[which])

                row_chunks(rows, add)

        for load in loads[1:]:
            load.start()
        saves = []

        def save(name):
            target = out[name]
            extent = buf[name].shape[0]
            copy = pltpu.make_async_copy(
                buf[name], target.at[pl.ds(index * extent, extent)], osem.at[len(saves)]
            )
            copy.start()
            saves.append(copy)

        save("x")

        def norm_one(at):
            unit, _ = unit_rows(x_ref[at, :])
            buf["a"][at, :] = (unit * gain[0:1, :] + bias[0:1, :]).astype(BF)

        row_chunks(rows, norm_one)
        save("a")
        loads[0].wait()
        for at in range(0, 3 * width, 256):
            buf["qkv"][:, at:at + 256] = mm(buf["a"][...], wqkv[:, at:at + 256]).astype(BF)
        save("qkv")

        row = lax.broadcasted_iota(jnp.int32, (2 * group, group), 0) % group
        col = lax.broadcasted_iota(jnp.int32, (2 * group, group), 1)
        if stride == 1:
            same = col // length == row // length
        else:
            same = col % stride == row % stride
        allowed = (col <= row) & same

        def attend(which, carry):
            at = pl.ds(pl.multiple_of(which * group, group), group)
            for pair in range(HEADS // 2):
                lanes = pair * 128
                queries = buf["qkv"][at, lanes:lanes + 128] * jnp.asarray(HEAD ** -0.5, BF)
                keys = buf["qkv"][at, width + lanes:width + lanes + 128]
                values = buf["qkv"][at, 2 * width + lanes:2 * width + lanes + 128]
                scores = jnp.where(allowed, mm(two_heads(queries), keys, NT), MASK_FILL)
                weight = jnp.exp(scores - jnp.max(scores, axis=-1, keepdims=True))
                chance = (weight / jnp.sum(weight, axis=-1, keepdims=True)).astype(BF)
                buf["p"][which * (HEADS // 2) + pair] = chance
                buf["o"][at, lanes:lanes + 128] = one_pair(mm(chance, values)).astype(BF)
            return carry

        lax.fori_loop(0, rows // group, attend, 0)
        save("p")
        save("o")
        loads[1].wait()
        for at in range(0, width, 256):
            buf["x2"][:, at:at + 256] = x_ref[:, at:at + 256] + mm(buf["o"][...], wout[:, at:at + 256])
        save("x2")

        def norm_two(at):
            unit, _ = unit_rows(buf["x2"][at, :])
            buf["c"][at, :] = (unit * gain[1:2, :] + bias[1:2, :]).astype(BF)

        row_chunks(rows, norm_two)
        save("c")
        loads[2].wait()
        for at in range(0, hidden, 256):
            pre = mm(buf["c"][...], wup[:, at:at + 256])
            square = pre * pre
            bent = jnp.tanh(ROOT * (pre + CUBE * square * pre))
            share = 0.5 * (1.0 + bent)
            buf["r"][:, at:at + 256] = (pre * share).astype(BF)
            slope = share + (0.5 * ROOT) * pre * (1.0 - bent * bent) * (1.0 + (3 * CUBE) * square)
            buf["gp"][:, at:at + 256] = slope.astype(BF)
        save("gp")
        save("r")
        loads[3].wait()
        for at in range(0, width, 256):
            y_ref[:, at:at + 256] = (
                buf["x2"][:, at:at + 256] + mm(buf["r"][...], wdown[:, at:at + 256])
            ).astype(BF)
        for copy in saves:
            copy.wait()


def block_fwd(ctrl, first, second, rows, gain, bias, weights, stored, total, length, stride, name):
    width, hidden = weights[2].shape
    shapes = stored_shapes(rows, width, hidden)
    times = total // rows
    full = [
        jax.ShapeDtypeStruct((shapes[k][0][0] * times,) + shapes[k][0][1:], shapes[k][1]) for k in STORED
    ]
    lead = 0 if stored is None else len(STORED)
    counts = (len(first), len(second))
    inputs = sum(counts)
    result = pl.pallas_call(
        functools.partial(fwd_kernel, rows, length, stride, counts, lead),
        out_shape=[jax.ShapeDtypeStruct((rows, width), BF)] + full,
        in_specs=[SM] + [ANY] * inputs + [VM, VM] + [ANY] * (4 + lead),
        out_specs=[VM] + [ANY] * len(STORED),
        scratch_shapes=[pltpu.VMEM(*shapes[k]) for k in STORED]
        + [pltpu.VMEM((rows, width), a.dtype) for a in (*first, *second)]
        + [pltpu.VMEM(w.shape, w.dtype) for w in weights]
        + [
            pltpu.SemaphoreType.DMA((max(counts),)),
            pltpu.SemaphoreType.DMA((4,)),
            pltpu.SemaphoreType.DMA((len(STORED),)),
        ],
        input_output_aliases={7 + inputs + i: 1 + i for i in range(lead)},
        compiler_params=pltpu.CompilerParams(vmem_limit_bytes=56 << 20),
        name=name,
    )(ctrl, *first, *second, gain, bias, *weights, *(() if stored is None else stored))
    return result[0], tuple(result[1:])


def norm_back_rows(grad, unit, inverse, gain_row):
    scaled = grad * gain_row
    return inverse * (
        scaled
        - jnp.mean(scaled, axis=-1, keepdims=True)
        - unit * jnp.mean(scaled * unit, axis=-1, keepdims=True)
    )


def bwd_kernel(rows, counts, lead, *refs):
    ctrl = refs[0]
    inputs = refs[1:1 + counts]
    refs = refs[1 + counts:]
    gain, wqkv_h, wout_h, wup_h, wdown_h = refs[:5]
    src = dict(zip(USED, refs[5:10]))
    refs = refs[10 + lead:]
    dx_ref, gn_ref = refs[:2]
    out = dict(zip(GRADS, refs[2:6]))
    buf = dict(zip(USED, refs[6:11]))
    grd = dict(zip(GRADS, refs[11:15]))
    do_s, dx2_s, wqkv, wout, wup, wdown, wsem, rsem, osem = refs[15:]
    dy_ref = grd["dz"]
    width = dx_ref.shape[1]
    hidden = wup.shape[1]
    group = min(rows, 128)

    @pl.when(ctrl[0] == 1)
    def run():
        index = ctrl[1]
        reads = {}

        def read(name, at):
            extent = buf[name].shape[0]
            reads[name] = pltpu.make_async_copy(
                src[name].at[pl.ds(index * extent, extent)], buf[name], rsem.at[at]
            )
            reads[name].start()

        loads = [
            pltpu.make_async_copy(wdown_h, wdown, wsem.at[0]),
            pltpu.make_async_copy(wup_h, wup, wsem.at[1]),
            pltpu.make_async_copy(wout_h, wout, wsem.at[2]),
            pltpu.make_async_copy(wqkv_h, wqkv, wsem.at[3]),
        ]
        for which in range(counts):

            @pl.when(ctrl[2] == which)
            def bring():
                pltpu.make_async_copy(own_rows(inputs[which], rows, index), dy_ref, wsem.at[4]).start()

        loads[0].start()
        read("gp", 0)
        loads[1].start()
        read("x2", 1)
        loads[2].start()
        read("qkv", 2)
        read("p", 3)
        loads[3].start()
        read("x", 4)
        saves = []

        def save(name):
            extent = grd[name].shape[0]
            copy = pltpu.make_async_copy(
                grd[name], out[name].at[pl.ds(index * extent, extent)], osem.at[len(saves)]
            )
            copy.start()
            saves.append(copy)

        pltpu.make_async_copy(own_rows(inputs[0], rows, index), dy_ref, wsem.at[4]).wait()
        save("dz")
        loads[0].wait()
        reads["gp"].wait()
        for at in range(0, hidden, 256):
            part = mm(dy_ref[...], wdown[at:at + 256, :], NT)
            grd["du"][:, at:at + 256] = (part * buf["gp"][:, at:at + 256].astype(F32)).astype(BF)
        save("du")
        loads[1].wait()
        reads["x2"].wait()
        for at in range(0, width, 256):
            dx2_s[:, at:at + 256] = mm(grd["du"][...], wup[at:at + 256, :], NT)
        gn_ref[...] = jnp.zeros_like(gn_ref)

        def back_two(at):
            unit, inverse = unit_rows(buf["x2"][at, :])
            grad = dx2_s[at, :]
            gn_ref[1:2, :] += jnp.sum(grad * unit, axis=0, keepdims=True)
            gn_ref[3:4, :] += jnp.sum(grad, axis=0, keepdims=True)
            mixed = dy_ref[at, :].astype(F32) + norm_back_rows(grad, unit, inverse, gain[1:2, :])
            dx2_s[at, :] = mixed
            grd["dA"][at, :] = mixed.astype(BF)

        row_chunks(rows, back_two)
        save("dA")
        loads[2].wait()
        for at in range(0, width, 256):
            do_s[:, at:at + 256] = mm(grd["dA"][...], wout[at:at + 256, :], NT).astype(BF)
        reads["qkv"].wait()
        reads["p"].wait()

        def attend(which, carry):
            at = pl.ds(pl.multiple_of(which * group, group), group)
            for pair in range(HEADS // 2):
                lanes = pair * 128
                queries = two_heads(buf["qkv"][at, lanes:lanes + 128] * jnp.asarray(HEAD ** -0.5, BF))
                keys = buf["qkv"][at, width + lanes:width + lanes + 128]
                values = buf["qkv"][at, 2 * width + lanes:2 * width + lanes + 128]
                grads = two_heads(do_s[at, lanes:lanes + 128])
                chance = buf["p"][which * (HEADS // 2) + pair]
                wide = chance.astype(F32)
                slope = mm(grads, values, NT)
                weighed = slope * wide
                total = jnp.sum(weighed, axis=-1, keepdims=True)
                scores = (weighed - wide * total).astype(BF)
                dq = one_pair(mm(scores, keys)) * HEAD ** -0.5
                dk = mm(scores, queries, TN)
                dv = mm(chance, grads, TN)
                grd["dqkv"][at, lanes:lanes + 128] = dq.astype(BF)
                grd["dqkv"][at, width + lanes:width + lanes + 128] = dk.astype(BF)
                grd["dqkv"][at, 2 * width + lanes:2 * width + lanes + 128] = dv.astype(BF)
            return carry

        lax.fori_loop(0, rows // group, attend, 0)
        save("dqkv")
        loads[3].wait()
        reads["x"].wait()
        for at in range(0, width, 256):
            buf["x2"][:, at:at + 256] = mm(grd["dqkv"][...], wqkv[at:at + 256, :], NT)

        def back_one(at):
            unit, inverse = unit_rows(buf["x"][at, :])
            grad = buf["x2"][at, :]
            gn_ref[0:1, :] += jnp.sum(grad * unit, axis=0, keepdims=True)
            gn_ref[2:3, :] += jnp.sum(grad, axis=0, keepdims=True)
            dx_ref[at, :] = (
                dx2_s[at, :] + norm_back_rows(grad, unit, inverse, gain[0:1, :])
            ).astype(BF)

        row_chunks(rows, back_one)
        for copy in saves:
            copy.wait()


def block_bwd(ctrl, inputs, rows, gain, weights, stored, grads, total, name):
    width, hidden = weights[2].shape
    shapes = stored_shapes(rows, width, hidden)
    pick = dict(zip(STORED, stored))
    gshape = {"dz": width, "du": hidden, "dA": width, "dqkv": 3 * width}
    lead = 0 if grads is None else len(GRADS)
    counts = len(inputs)
    result = pl.pallas_call(
        functools.partial(bwd_kernel, rows, counts, lead),
        out_shape=[jax.ShapeDtypeStruct((rows, width), BF), jax.ShapeDtypeStruct((8, width), F32)]
        + [jax.ShapeDtypeStruct((total, gshape[k]), BF) for k in GRADS],
        in_specs=[SM] + [ANY] * counts + [VM, ANY, ANY, ANY, ANY] + [ANY] * (len(USED) + lead),
        out_specs=[VM, VM] + [ANY] * len(GRADS),
        scratch_shapes=[pltpu.VMEM(*shapes[k]) for k in USED]
        + [pltpu.VMEM((rows, gshape[k]), BF) for k in GRADS]
        + [pltpu.VMEM((rows, width), BF), pltpu.VMEM((rows, width), F32)]
        + [pltpu.VMEM(w.shape, w.dtype) for w in weights]
        + [
            pltpu.SemaphoreType.DMA((5,)),
            pltpu.SemaphoreType.DMA((len(USED),)),
            pltpu.SemaphoreType.DMA((len(GRADS),)),
        ],
        input_output_aliases={11 + counts + i: 2 + i for i in range(lead)},
        compiler_params=pltpu.CompilerParams(vmem_limit_bytes=56 << 20),
        name=name,
    )(ctrl, *inputs, gain, *weights, *(pick[k] for k in USED), *(() if grads is None else grads))
    return result[0], result[1], tuple(result[2:])


def product_kernel(place_ref, left, right, mine, theirs, whole, sems):
    extent = mine.shape[1]
    depth, wide = whole.shape
    copies = []
    step = 256 if depth > wide else 128
    ready = 0
    for at in range(0, depth, step):
        whole[at:at + step, :] = mm(left[:, at:at + step], right[...], TN).astype(BF)
        while (ready + 1) * extent <= at + step:
            source = whole.at[pl.ds(ready * extent, extent)]
            other = place_ref[0] ^ ready
            to_mine = pltpu.make_async_copy(source, mine.at[other >> 1], sems.at[ready])
            to_theirs = pltpu.make_async_copy(source, theirs.at[other >> 1], sems.at[ready])
            same = (other & 1) == 0
            pl.when(same)(to_mine.start)
            pl.when(jnp.logical_not(same))(to_theirs.start)
            copies.append(to_mine)
            ready += 1
    for copy in copies:
        copy.wait()


def products(place, left, right, shards, name):
    depth, wide = left.shape[1], right.shape[1]
    half = jax.ShapeDtypeStruct((shards // 2, depth // shards, wide), BF)
    return pl.pallas_call(
        product_kernel,
        out_shape=[half, half],
        in_specs=[SM, VM, VM],
        out_specs=[ANY, ANY],
        scratch_shapes=[pltpu.VMEM((depth, wide), BF), pltpu.SemaphoreType.DMA((shards,))],
        compiler_params=pltpu.CompilerParams(vmem_limit_bytes=48 << 20),
        name=name,
    )(place, left, right)


MASKS = (0, 2, 4, 6, 1, 3, 5, 7)


def share_kernel(place, patches, *refs):
    pieces, (own, sent) = refs[:-2], refs[-2:]
    total = sum(mm(patches[place[0] ^ mask], piece[...]) for mask, piece in zip(MASKS, pieces))
    own[...] = total
    sent[...] = total.astype(BF)


def entry_share(place, patches, pieces):
    extent = (patches.shape[1], pieces[0].shape[1])
    return pl.pallas_call(
        share_kernel,
        out_shape=[jax.ShapeDtypeStruct(extent, F32), jax.ShapeDtypeStruct(extent, BF)],
        in_specs=[SM] + [VM] * (1 + len(pieces)),
        out_specs=[VM, VM],
        compiler_params=pltpu.CompilerParams(vmem_limit_bytes=32 << 20),
        name="entry_share",
    )(place, patches, *pieces)


def input_kernel(place, start, *refs):
    pieces, out, parts = refs[:-2], refs[-2], refs[-1]
    for at, piece in enumerate(pieces):
        parts[place[0] ^ MASKS[at]] = mm(start[...], piece[...], NT).astype(BF)
    per = len(pieces) // out.shape[0]
    for byte in range(out.shape[0]):
        out[byte] = jnp.concatenate([parts[byte * per + at] for at in range(per)], axis=1)


def input_share(place, start, pieces, count):
    rows, width = start.shape
    return pl.pallas_call(
        input_kernel,
        out_shape=jax.ShapeDtypeStruct((count, rows, width), BF),
        in_specs=[SM] + [VM] * (1 + len(pieces)),
        out_specs=VM,
        scratch_shapes=[pltpu.VMEM((len(pieces), rows, pieces[0].shape[0]), BF)],
        compiler_params=pltpu.CompilerParams(vmem_limit_bytes=32 << 20),
        name="input_share",
    )(place, start, *pieces)


def hold_pieces(pieces, held, sems):
    copies = [pltpu.make_async_copy(piece, held.at[at], sems.at[at]) for at, piece in enumerate(pieces)]
    for copy in copies:
        copy.start()
    return copies


def bridge_forward_kernel(shape, ctrl, summary, embedded, *refs):
    sections, shards, extent, items, patches = shape
    pieces, entered, held, parts, sems = refs[:shards], refs[shards], refs[-3], refs[-2], refs[-1]
    step = held.shape[1] // sections
    per = summary.shape[1] // extent

    @pl.when(ctrl[0] == 1)
    def run():
        copies = hold_pieces(pieces, held, sems)
        for at, copy in enumerate(copies):
            copy.wait()
            for section in range(sections):
                weight = held[at, section * step:section * step + extent, :]
                parts[section * shards + (ctrl[1] ^ MASKS[at])] = mm(summary[...], weight, NT)
        for byte in range(sections * shards // per):
            block = jnp.concatenate([parts[byte * per + at] for at in range(per)], axis=1)
            for item in range(items):
                at = (item * PATCH + byte) * patches
                lines = slice(at, at + patches)
                entered[lines, :] = embedded[lines, :].astype(F32) + block[item * patches:(item + 1) * patches]


def bridge_forward(ctrl, summary, embedded, pieces, sections, extent, items):
    shards, patches = len(pieces), summary.shape[0] // items
    shape = (sections, shards, extent, items, patches)
    return pl.pallas_call(
        functools.partial(bridge_forward_kernel, shape),
        out_shape=jax.ShapeDtypeStruct(embedded.shape, F32),
        in_specs=[SM, VM, VM] + [ANY] * shards,
        out_specs=VM,
        scratch_shapes=[
            pltpu.VMEM((shards,) + pieces[0].shape, BF),
            pltpu.VMEM((sections * shards, summary.shape[0], extent), F32),
            pltpu.SemaphoreType.DMA((shards,)),
        ],
        compiler_params=pltpu.CompilerParams(vmem_limit_bytes=48 << 20),
        name="bridge_forward",
    )(ctrl, summary, embedded, *pieces)


def bridge_backward_kernel(shape, ctrl, *refs):
    sections, shards, extent, items, patches, chunks = shape
    entries, refs = refs[:chunks], refs[chunks:]
    pieces, refs = refs[:shards], refs[shards:]
    back, slopes, (held, parts, sems) = refs[0], refs[1:1 + sections], refs[1 + sections:]
    step = held.shape[1] // sections
    per = back.shape[1] // extent

    @pl.when(ctrl[0] == 1)
    def run():
        copies = hold_pieces(pieces, held, sems)
        for byte in range(sections * shards // per):
            lines = []
            for item in range(items):
                at = (item * PATCH + byte) * patches
                entry = entries[at // entries[0].shape[0]]
                at = at % entries[0].shape[0]
                lines.append(entry[at:at + patches, :])
            block = jnp.concatenate(lines, axis=0)
            for at in range(per):
                parts[byte * per + at] = block[:, at * extent:(at + 1) * extent]
        total = 0.0
        for at, copy in enumerate(copies):
            copy.wait()
            for section in range(sections):
                left = parts[section * shards + (ctrl[1] ^ MASKS[at])]
                slopes[section][ctrl[1] ^ MASKS[at]] = left
                total = total + mm(left, held[at, section * step:section * step + extent, :])
        back[...] = total.astype(BF)


def bridge_backward(ctrl, entries, pieces, sections, extent, items, small):
    shards, width = len(pieces), entries[0].shape[1]
    shape = (sections, shards, extent, items, small // items, len(entries))
    result = pl.pallas_call(
        functools.partial(bridge_backward_kernel, shape),
        out_shape=[jax.ShapeDtypeStruct((small, width), BF)]
        + [jax.ShapeDtypeStruct((shards, small, extent), BF)] * sections,
        in_specs=[SM] + [VM] * len(entries) + [ANY] * shards,
        out_specs=[VM] * (1 + sections),
        scratch_shapes=[
            pltpu.VMEM((shards,) + pieces[0].shape, BF),
            pltpu.VMEM((sections * shards, small, extent), BF),
            pltpu.SemaphoreType.DMA((shards,)),
        ],
        compiler_params=pltpu.CompilerParams(vmem_limit_bytes=48 << 20),
        name="bridge_backward",
    )(ctrl, *entries, *pieces)
    return result[0], list(result[1:])


def slice_products_kernel(spans, left, *refs):
    count = len(spans)
    pieces, outs, held, sems = refs[:-2 - count], refs[-2 - count:-2], refs[-2], refs[-1]
    rows = held.shape[0] // len(pieces)
    copies = [
        pltpu.make_async_copy(piece, held.at[pl.ds(at * rows, rows)], sems.at[at])
        for at, piece in enumerate(pieces)
    ]
    for copy in copies:
        copy.start()
    for copy in copies:
        copy.wait()
    for (first, extent, column, wide), out in zip(spans, outs):
        room = -(-extent // 128) * 128
        for at in range(0, wide, 768):
            part = mm(left[:, first:first + room], held[:, column + at:column + at + 768], TN)
            out[:, at:at + 768] = part[:extent]


def slice_products(left, pieces, spans, name):
    rows = sum(piece.shape[0] for piece in pieces)
    return pl.pallas_call(
        functools.partial(slice_products_kernel, spans),
        out_shape=[jax.ShapeDtypeStruct((span[1], span[3]), F32) for span in spans],
        in_specs=[VM] + [ANY] * len(pieces),
        out_specs=[VM] * len(spans),
        scratch_shapes=[
            pltpu.VMEM((rows, pieces[0].shape[1]), BF),
            pltpu.SemaphoreType.DMA((len(pieces),)),
        ],
        compiler_params=pltpu.CompilerParams(vmem_limit_bytes=48 << 20),
        name=name,
    )(left, *pieces)


def swap(block, mask):
    if mask == 0:
        return block
    shards = lax.axis_size("dp")
    return lax.ppermute(block, "dp", [(i, i ^ mask) for i in range(shards)])


def gather_pieces(block):
    same = [swap(block, mask) for mask in MASKS[:4]]
    return same + [swap(piece, 1) for piece in same]


def exchange_pieces(pieces):
    return [swap(piece, mask) for piece, mask in zip(pieces, MASKS)]


def by_mask(blocks, place, back=False):
    count = blocks.shape[0]
    if back:
        blocks = jnp.stack([blocks[MASKS.index(mask)] for mask in range(count)])
    bit = 1
    while bit < count:
        halves = blocks.reshape((count // (2 * bit), 2, bit) + blocks.shape[1:])
        blocks = jnp.where((place & bit) != 0, halves[:, ::-1], halves).reshape(blocks.shape)
        bit *= 2
    return blocks if back else jnp.stack([blocks[mask] for mask in MASKS])


def reduce_shards(pair):
    mine, theirs = pair
    came = swap(theirs, 1)
    half = mine.shape[1] // 2

    def first(mask, lower):
        lines = slice(0, half) if lower else slice(half, None)
        return mine[mask, lines].astype(F32) + came[mask, lines].astype(F32)

    lows = swap(jnp.stack([first(1, True), first(3, True)]).astype(BF), 2)
    highs = swap(jnp.stack([first(2, False), first(3, False)]).astype(BF), 4)
    low = swap((first(2, True) + lows[1].astype(F32)).astype(BF), 4)
    high = swap((first(1, False) + highs[1].astype(F32)).astype(BF), 2)
    return jnp.concatenate(
        [
            first(0, True) + lows[0].astype(F32) + low.astype(F32),
            first(0, False) + highs[0].astype(F32) + high.astype(F32),
        ],
        axis=0,
    )


def hop(block, source, target):
    return lax.ppermute(block, "section", [(source, target)])


def own_entry(blocks, rank, source):
    result = blocks[source]
    for section in range(len(blocks)):
        if section != source:
            result = jnp.where(rank == section, hop(blocks[section], source, section), result)
    return result


def after(value, *others):
    return lax.optimization_barrier((value, *others))[0]


def control(*values):
    return jnp.stack([jnp.asarray(v, jnp.int32) for v in values])


def on_device(
    byte_input,
    byte_ids,
    valid_bytes,
    norm_gain,
    norm_bias,
    w_qkv,
    w_out,
    w_up,
    w_down,
    patch_proj,
    bridge,
    byte_table,
    cotangent,
):
    rank = lax.axis_index("section")
    place = lax.axis_index("dp")
    sections = lax.axis_size("section")
    shards = lax.axis_size("dp")
    items, byte_count, width = byte_input.shape
    hidden = w_up.shape[2]
    patch_count = byte_count // PATCH
    rows = items * byte_count
    small = items * patch_count
    gain, bias = norm_gain[0], norm_bias[0]
    weights = (w_qkv[0], w_out[0], w_up[0], w_down[0])
    half, last = sections // 2, sections - 1
    is_first, is_second, is_bridge, is_last = rank == 0, rank == 1, rank == half, rank == last
    is_global = rank < half
    parts = 2 if items % 2 == 0 else 1
    chunk = rows // parts
    own_bytes = PATCH // sections
    extent = patch_proj.shape[0]
    per = byte_table.shape[0]
    wide = {"r": hidden, "du": hidden, "dqkv": 3 * width}
    joint = ("section", "dp")
    spot = place.reshape(1).astype(jnp.int32)

    def between(source, target):
        return [(source * shards + i, target * shards + i) for i in range(shards)]

    def blank(*shape, kind=BF):
        return jnp.zeros(shape, kind)

    patch_pieces = gather_pieces(patch_proj)
    own_patches = lax.dynamic_slice_in_dim(
        byte_input.reshape(small, PATCH, width), rank * own_bytes, own_bytes, 1
    )
    own_patches = own_patches.reshape(small, shards, extent).transpose(1, 0, 2)
    patch_columns = lax.all_to_all(own_patches, "dp", 0, 0, tiled=True)
    share, sent = entry_share(spot, own_patches, patch_pieces)
    starts = [hop(sent, source, 0) for source in range(1, sections)]

    entry_rows = jnp.concatenate([bridge, byte_table, blank(per, width)], axis=0)
    entry_rows = jnp.concatenate([entry_rows if s == half else hop(entry_rows, s, half) for s in range(sections)])
    step = entry_rows.shape[0] // sections

    def by_byte(block):
        shaped = block.reshape((items, patch_count, PATCH) + block.shape[2:])
        return jnp.swapaxes(shaped, 1, 2)

    def global_forward(operands):
        starts, entry_rows, byte_ids, cotangent = operands
        first_out, kept = block_fwd(
            control(is_first, 0, 0), starts, [], small, gain, bias, weights, None, small, patch_count, 1, "global_fwd_one"
        )
        nothing = after(jnp.zeros((), BF), first_out)
        received = lax.ppermute(first_out, joint, between(0, 1))
        second_out, kept = block_fwd(
            control(is_second, 0, 0),
            [received],
            [],
            small,
            gain,
            bias,
            weights,
            kept,
            small,
            patch_count,
            1,
            "global_fwd_two",
        )
        pieces = tuple(jnp.broadcast_to(nothing, (sections * step, width)) for _ in MASKS)
        one_hot, embedded, target = [jnp.broadcast_to(nothing, (rows, c)) for c in (VOCAB, width, width)]
        return second_out, kept, pieces, one_hot, embedded, target

    def local_inputs(operands):
        starts, entry_rows, byte_ids, cotangent = operands
        pieces = gather_pieces(entry_rows)
        tables = [p.reshape(sections, step, width)[:, extent:extent + per] for p in pieces]
        table = jnp.stack(tables).reshape(VOCAB, width)
        spots = [(s * shards + (place ^ mask)) * per for mask in MASKS for s in range(sections)]
        ids = jnp.concatenate([spot + jnp.arange(per, dtype=jnp.int32) for spot in spots])
        read = by_byte(byte_ids)
        read = jnp.concatenate([jnp.full_like(read[:, :1], -1), read[:, :-1]], axis=1).reshape(rows)
        one_hot = (read[:, None] == ids[None, :]).astype(BF)
        positions = lax.broadcasted_iota(jnp.int32, (items, byte_count), 1)
        keep = by_byte((positions < valid_bytes[:, None]).astype(BF)).reshape(rows, 1)
        target = by_byte(cotangent).reshape(rows, width) * keep
        shapes = stored_shapes(small, width, hidden)
        kept = tuple(blank(*shapes[k][0], kind=shapes[k][1]) for k in STORED)
        return blank(small, width), kept, tuple(pieces), one_hot, mm(one_hot, table).astype(BF), target

    second_out, global_store, pieces, one_hot, embedded, target = lax.cond(
        is_global, global_forward, local_inputs, ([share, *starts], entry_rows, byte_ids, cotangent)
    )
    summary_hop = hop(second_out, 1, half)
    entered = bridge_forward(
        control(is_bridge, place), summary_hop, embedded, pieces, sections, extent, items
    )
    others = after(second_out, summary_hop)
    summary = jnp.where(
        is_second,
        second_out,
        summary_hop + sum(hop(others, 1, s) for s in range(sections) if s not in (1, half)),
    )

    def local_blocks(operands):
        entered, target, store = operands
        store, grads = None, None
        finals, entries, norms = [], [], []
        coming = blank(chunk, width)
        back = blank(chunk, width)
        for tick in range(parts + 2):
            if tick <= parts:
                active = (is_bridge & (tick < parts)) | (is_last & (tick >= 1))
                index = jnp.where(is_last, tick - 1, tick)
                result, store = block_fwd(
                    control(active, index, is_last),
                    [entered],
                    [coming],
                    chunk,
                    gain,
                    bias,
                    weights,
                    store,
                    rows,
                    PATCH,
                    patch_count,
                    "local_fwd_%d" % tick,
                )
                if tick < parts:
                    coming = lax.ppermute(result, joint, between(half, last))
                if tick >= 1:
                    finals.append(result)
            if tick >= 1:
                active = (is_last & (tick <= parts)) | (is_bridge & (tick >= 2))
                index = jnp.where(is_last, tick - 1, tick - 2)
                result, norm, grads = block_bwd(
                    control(active, index, is_bridge),
                    [target, back],
                    chunk,
                    gain,
                    weights,
                    store,
                    grads,
                    rows,
                    "local_bwd_%d" % tick,
                )
                norms.append(jnp.where(active, norm, 0.0))
                store, result = lax.optimization_barrier((store, result))
                if tick <= parts:
                    back = lax.ppermute(result, joint, between(last, half))
                if tick >= 2:
                    entries.append(result)

        def share_out(finals):
            positions = lax.broadcasted_iota(jnp.int32, (items, byte_count), 1)
            keep = (positions < valid_bytes[:, None]).astype(BF)
            final = jnp.concatenate(finals, axis=0).reshape(items, PATCH, patch_count, width)
            final = jnp.swapaxes(final, 1, 2).reshape(items, byte_count, width) * keep[..., None]
            final = final.reshape(items, sections, byte_count // sections, width)
            return tuple(final[:, s] for s in range(sections))

        def share_none(finals):
            return tuple(blank(items, byte_count // sections, width) for s in range(sections))

        mixed = lax.cond(is_last, share_out, share_none, finals)
        pick = dict(zip(STORED, store))
        return mixed, tuple(entries), sum(norms), tuple(pick[k] for k in KEPT), grads, blank(shards * small, width)

    def local_idle(operands):
        entered, target, store = operands
        pick = dict(zip(STORED, store))
        columns = []
        for key in KEPT:
            block = pick[key].reshape(small, shards, -1)
            room = -block.shape[2] % 128
            columns.append(jnp.pad(block, ((0, 0), (0, 0), (0, room))))
        columns = by_mask(jnp.concatenate(columns, axis=2).transpose(1, 0, 2), place)
        columns = jnp.concatenate(exchange_pieces([columns[at] for at in range(shards)]), axis=0)
        return (
            tuple(blank(items, byte_count // sections, width) for s in range(sections)),
            tuple(blank(chunk, width) for _ in range(parts)),
            blank(8, width, kind=F32),
            tuple(blank(rows, wide.get(k, width)) for k in KEPT),
            tuple(blank(rows, wide.get(k, width)) for k in GRADS),
            columns,
        )

    mixed, entries, norm, local_kept, local_slopes, kept_columns = lax.cond(
        is_global, local_idle, local_blocks, (entered, target, global_store)
    )

    summary_back, slopes = bridge_backward(
        control(is_bridge, place), entries, pieces, sections, extent, items, small
    )
    arriving = hop(summary_back, half, 1)

    def weight_grad(key, slope_key):
        left = dict(zip(KEPT, local_kept))[key]
        right = dict(zip(GRADS, local_slopes))[slope_key]
        return products(spot, left, right, shards, "weight_grad_" + key)

    room = {"r": 0, "c": hidden // shards}
    room["o"] = room["c"] + -(-(width // shards) // 128) * 128
    room["a"] = room["o"] + -(-(width // shards) // 128) * 128

    def global_backward(operands):
        arriving, norm, one_hot, entries, kept_columns = operands
        second_back, norm_two, grads = block_bwd(
            control(is_second, 0, 0), [arriving], small, gain, weights, global_store, None, small, "global_bwd_two"
        )
        nothing = after(jnp.zeros((), BF), second_back)
        coming = lax.ppermute(second_back, joint, between(1, 0))
        start_back, norm_one, grads = block_bwd(
            control(is_first, 0, 0), [coming], small, gain, weights, global_store, grads, small, "global_bwd_one"
        )
        norm = jnp.where(is_first, norm_one, jnp.where(is_second, norm_two, 0.0))
        slopes = dict(zip(GRADS, grads))
        right = gather_pieces(jnp.concatenate([slopes["dz"], slopes["du"]], axis=1))
        spans = ((room["r"], hidden // shards, 0, width), (room["c"], width // shards, width, hidden))
        first = slice_products(kept_columns, right, spans, "slice_grads_one")
        right = gather_pieces(jnp.concatenate([slopes["dA"], slopes["dqkv"]], axis=1))
        spans = ((room["o"], width // shards, 0, width), (room["a"], width // shards, width, 3 * width))
        made = (*first, *slice_products(kept_columns, right, spans, "slice_grads_two"))
        return start_back, norm, jnp.broadcast_to(nothing, (sections, shards, per, width)), made

    def local_weights(operands):
        arriving, norm, one_hot, entries, kept_columns = operands
        pairs = (("r", "dz"), ("c", "du"), ("o", "dA"), ("a", "dqkv"))
        made = [weight_grad(*pair) for pair in pairs]
        table_part = mm(one_hot, jnp.concatenate(entries, axis=0), TN).astype(BF)
        table_part = jnp.swapaxes(table_part.reshape(shards, sections, per, width), 0, 1)
        return blank(small, width), norm, table_part, tuple(reduce_shards(pair) for pair in made)

    start_back, norm, table_part, made = lax.cond(
        is_global, global_backward, local_weights, (arriving, norm, one_hot, entries, kept_columns)
    )
    made_r, made_c, made_o, made_a = made
    norm_sum = lax.psum_scatter(norm[:4], "dp", scatter_dimension=1, tiled=True)
    start_all = jnp.where(is_first, start_back, sum(hop(start_back, 0, s) for s in range(1, sections)))
    start_everywhere = lax.all_to_all(
        jnp.broadcast_to(start_all[None], (shards, small, width)), "dp", 0, 0, tiled=True
    )
    inputs = input_share(spot, start_all, patch_pieces, own_bytes)
    inputs = inputs.reshape(own_bytes, items, sections, patch_count // sections, width).transpose(2, 1, 3, 0, 4)
    turned = []
    for turn in range(sections):
        block = lax.dynamic_index_in_dim(inputs, (rank + turn) % sections, 0, keepdims=False)
        if turn:
            block = lax.ppermute(block, "section", [(s, (s + turn) % sections) for s in range(sections)])
        turned.append(block)

    table_part = own_entry(table_part, rank, half)
    mixed, slopes = after((mixed, slopes), start_back)
    slope = own_entry(slopes, rank, half)
    mixed = own_entry(mixed, rank, last)
    packed = jnp.concatenate(
        [
            slope,
            by_mask(table_part, place, True).reshape(shards, -1, extent),
            jnp.broadcast_to(summary.reshape(1, -1, extent), (shards, small * width // extent, extent)),
        ],
        axis=1,
    )
    packed = lax.all_to_all(packed, "dp", 0, 0, tiled=True)
    columns = packed[:, :small].reshape(shards * small, extent)
    tables = packed[:, small:small + per * width // extent]
    everywhere = packed[:, small + per * width // extent:].reshape(shards * small, width)
    grad_bridge = mm(columns, everywhere, TN)
    grad_table = jnp.sum(tables.astype(F32), axis=0).reshape(per, width)
    grad_patch = mm(
        patch_columns.reshape(shards * small, extent), start_everywhere.reshape(shards * small, width), TN
    )

    turned = jnp.stack(turned)
    grad_input = jnp.stack(
        [lax.dynamic_index_in_dim(turned, (rank - s) % sections, 0, keepdims=False) for s in range(sections)], axis=2
    )
    grad_input = grad_input.reshape(items, byte_count // sections, width).astype(F32)
    return (
        mixed,
        grad_input,
        norm_sum[None, 0:2],
        norm_sum[None, 2:4],
        made_a[None],
        made_o[None],
        made_c[None],
        made_r[None],
        grad_patch,
        grad_bridge,
        grad_table,
    )


def on_any_device(
    byte_input,
    byte_ids,
    valid_bytes,
    norm_gain,
    norm_bias,
    w_qkv,
    w_out,
    w_up,
    w_down,
    patch_proj,
    bridge,
    byte_table,
    cotangent,
):
    rank = lax.axis_index("section")
    sections = lax.axis_size("section")
    items, byte_count, width = byte_input.shape
    patch_count = byte_count // PATCH
    rows = items * byte_count
    small = items * patch_count
    gain, bias = norm_gain[0], norm_bias[0]
    weights = (w_qkv[0], w_out[0], w_up[0], w_down[0])
    half, last = sections // 2, sections - 1
    is_first, is_second, is_bridge, is_last = rank == 0, rank == 1, rank == half, rank == last
    joint = ("section", "dp")

    def whole(block):
        return lax.all_gather(block, joint, axis=0, tiled=True)

    def by_byte(block):
        shaped = block.reshape((items, patch_count, PATCH) + block.shape[2:])
        return jnp.swapaxes(shaped, 1, 2)

    patch_rows, bridge_rows, table = whole(patch_proj), whole(bridge), whole(byte_table)
    ids = by_byte(byte_ids)
    before = jnp.concatenate([jnp.full_like(ids[:, :1], -1), ids[:, :-1]], axis=1).reshape(rows)
    one_hot = (before[:, None] == lax.broadcasted_iota(jnp.int32, (rows, VOCAB), 1)).astype(BF)
    positions = lax.broadcasted_iota(jnp.int32, (items, byte_count), 1)
    keep = by_byte((positions < valid_bytes[:, None]).astype(BF)).reshape(rows, 1)
    target = by_byte(cotangent).reshape(rows, width) * keep
    patches = byte_input.reshape(small, PATCH * width)

    def global_fwd(active, inputs, kept, name):
        return block_fwd(
            control(active, 0, 0), [inputs], [], small, gain, bias, weights, kept, small, patch_count, 1, name
        )

    def local_fwd(active, inputs, kept, name):
        return block_fwd(
            control(active, 0, 0), [inputs], [], rows, gain, bias, weights, kept, rows, PATCH, patch_count, name
        )

    first_out, global_store = global_fwd(is_first, mm(patches, patch_rows), None, "global_fwd_one")
    second_out, global_store = global_fwd(is_second, hop(first_out, 0, 1), global_store, "global_fwd_two")
    summary = hop(second_out, 1, half)
    projected = mm(summary, bridge_rows, NT).reshape(items, patch_count, PATCH, width)
    entered = mm(one_hot, table) + jnp.swapaxes(projected, 1, 2).reshape(rows, width)
    third_out, local_store = local_fwd(is_bridge, entered, None, "local_fwd_one")
    final, local_store = local_fwd(is_last, hop(third_out, half, last), local_store, "local_fwd_two")

    def back(active, slope, kept, grads, name):
        count = slope.shape[0]
        result, norm, grads = block_bwd(
            control(active, 0, 0), [slope], count, gain, weights, kept, grads, count, name
        )
        return result, jnp.where(active, norm, 0.0), grads

    third_back, norm_four, local_grads = back(is_last, target, local_store, None, "local_bwd_two")
    entry, norm_three, local_grads = back(
        is_bridge, hop(third_back, last, half), local_store, local_grads, "local_bwd_one"
    )
    entry = jnp.where(is_bridge, entry, jnp.zeros_like(entry))
    entry_rows = jnp.swapaxes(entry.reshape(items, PATCH, patch_count, width), 1, 2).reshape(small, PATCH * width)
    summary_back = mm(entry_rows, bridge_rows).astype(BF)
    first_back, norm_two, global_grads = back(
        is_second, hop(summary_back, half, 1), global_store, None, "global_bwd_two"
    )
    start_back, norm_one, global_grads = back(
        is_first, hop(first_back, 1, 0), global_store, global_grads, "global_bwd_one"
    )
    start_back = jnp.where(is_first, start_back, jnp.zeros_like(start_back))

    def weight_grads(stored, grads):
        pick, grads = dict(zip(STORED, stored)), dict(zip(GRADS, grads))
        pairs = (("a", "dqkv"), ("o", "dA"), ("c", "du"), ("r", "dz"))
        return tuple(mm(pick[a], grads[b], TN).astype(BF) for a, b in pairs)

    made = lax.cond(
        rank < half, lambda: weight_grads(global_store, global_grads), lambda: weight_grads(local_store, local_grads)
    )
    made = [lax.psum_scatter(m, "dp", scatter_dimension=0, tiled=True).astype(F32)[None] for m in made]
    norm = norm_one + norm_two + norm_three + norm_four
    norm_sum = lax.psum_scatter(norm[:4], "dp", scatter_dimension=1, tiled=True)

    def scattered(block):
        return lax.psum_scatter(block, joint, scatter_dimension=0, tiled=True)

    grad_bridge = scattered(mm(entry_rows, jnp.where(is_bridge, summary, jnp.zeros_like(summary)), TN))
    grad_table = scattered(mm(one_hot, entry, TN))
    grad_patch = scattered(mm(patches, start_back, TN))
    inputs = mm(start_back, patch_rows, NT).astype(BF).reshape(items, byte_count, width)
    grad_input = lax.psum_scatter(inputs, "section", scatter_dimension=1, tiled=True).astype(F32)
    mixed = jnp.swapaxes((final * keep).reshape(items, PATCH, patch_count, width), 1, 2)
    mixed = jnp.where(is_last, mixed, jnp.zeros_like(mixed)).reshape(items, byte_count, width)
    mixed = lax.psum_scatter(mixed, "section", scatter_dimension=1, tiled=True)
    return (
        mixed,
        grad_input,
        norm_sum[None, 0:2],
        norm_sum[None, 2:4],
        *made,
        grad_patch,
        grad_bridge,
        grad_table,
    )


def solution(mesh):
    return jax.shard_map(
        on_device if mesh.shape["dp"] == len(MASKS) else on_any_device,
        mesh=mesh,
        in_specs=(
            P("dp", None, None),
            P("dp", None),
            P("dp"),
            P("section", None, None),
            P("section", None, None),
            P("section", None, None),
            P("section", None, None),
            P("section", None, None),
            P("section", None, None),
            P(("section", "dp"), None),
            P(("section", "dp"), None),
            P(("section", "dp"), None),
            P("dp", None, None),
        ),
        out_specs=(
            P("dp", "section", None),
            P("dp", "section", None),
            P("section", None, "dp"),
            P("section", None, "dp"),
            P("section", "dp", None),
            P("section", "dp", None),
            P("section", "dp", None),
            P("section", "dp", None),
            P(("section", "dp"), None),
            P(("section", "dp"), None),
            P(("section", "dp"), None),
        ),
        check_vma=False,
    )
```
